32 devices in a mesh: group: 4 (over y, x), dp: 4 (over z), tensor: 2 (over core).
Axes of the slice: x: 2, y: 2, z: 4, core: 2. Of those that a mesh axis runs over, the one named last changes fastest.
Arguments:
- hidden: bfloat16 [2048, 8192], P(('group', 'tensor'), 'dp'), may hold values from -6 to 6
- out_weight: bfloat16 [8192, 8192], P('dp', 'tensor'), may hold values from -0.0625 to 0.0625
- out_bias: bfloat16 [8192], P('tensor'), may hold values from -3 to 3
- text_embeds: bfloat16 [10240, 8192], P(('group', 'dp'), 'tensor'), may hold values from -6 to 6
- image_rows: int32 [16, 4], P(('group', 'dp')), may hold values from 1 to 64, as said below
- image_group: int32 [16, 4], P(('group', 'dp')), may hold values from 0 to 3, as said below
- image_offset: int32 [16, 4], P(('group', 'dp')), may hold values from 1 to 576, as said below
Outputs:
- embeds: bfloat16 [10240, 8192], P(('group', 'dp'), 'tensor')
The draws below stay inside these ranges and needn't reach their ends.
Inputs may be any that keep to these rules, and one draw needn't show every extreme that they name: `image_rows`: each replica's image row counts sum to 128, and each replica has one image of exactly 64 rows. `image_group`: a replica's 4 images go to 4 distinct groups; on every dp index, one group receives a 64-row image from every group. `image_offset`: the images placed in one sequence don't intersect and lie within its 640 tokens; on every dp index some image starts at token 576.
All inputs are finite; a program needn't handle non-finite values.
Results may differ from the reference program's by a relative error of at most 0.0065.
Values may be sent and summed in bfloat16 or wider, within the bound.
A program may use at most 128 MiB of HBM per device.

```python
import jax
import jax.numpy as jnp
from jax import lax

D = 8192
ROW_DEV = 128
CAP = 64
TOK_DEV = 640
VROWS = 2048
TOKENS = 10240
N_GROUP = 4
N_DP = 4


def reorder_table(table, shuffle):
    return jnp.take_along_axis(table, shuffle, axis=-1).reshape(N_GROUP * N_DP, N_GROUP).astype(jnp.int32)


def plan_images(key):
    subkeys = jax.random.split(jax.random.fold_in(key, 101), 6)
    grid_shape = (N_GROUP, N_DP)
    low_cut = jax.random.randint(subkeys[0], grid_shape, 1, CAP // 2)
    high_cut = jax.random.randint(subkeys[1], grid_shape, CAP // 2, CAP)
    biggest = jnp.full(grid_shape, CAP, jnp.int32)
    sizes_raw = jnp.stack([biggest, low_cut, high_cut - low_cut, CAP - high_cut], axis=-1).astype(jnp.int32)
    big_group = jax.random.randint(subkeys[2], (N_DP,), 0, N_GROUP)
    rotation_scores = jax.random.randint(subkeys[3], (N_GROUP, N_DP, N_GROUP - 1), 0, 1 << 20) * 4 + jnp.arange(N_GROUP - 1)
    rotation = jnp.argsort(rotation_scores, axis=-1, stable=True).astype(jnp.int32)
    big_target = jnp.broadcast_to(big_group[None, :, None], (N_GROUP, N_DP, 1)).astype(jnp.int32)
    groups_raw = jnp.concatenate([big_target, (big_target + 1 + rotation) % N_GROUP], axis=-1).astype(jnp.int32)
    text_gaps = jax.random.randint(subkeys[4], (N_GROUP, N_DP, N_GROUP), 1, 3 * ROW_DEV // 4 + 1)
    landing = (groups_raw[:, :, :, None] == jnp.arange(N_GROUP)[None, None, None, :]).astype(jnp.int32)
    size_to = jnp.sum(landing * sizes_raw[:, :, :, None], axis=2)
    span_tokens = text_gaps + size_to
    total_span = jnp.sum(span_tokens, axis=0)
    is_big = jnp.arange(N_GROUP)[None, :] == big_group[:, None]
    shift = jnp.where(is_big, TOK_DEV - total_span, 0).astype(jnp.int32)
    offset_to = jnp.cumsum(span_tokens, axis=0) - size_to + shift[None, :, :]
    offsets_raw = jnp.sum(landing * offset_to[:, :, None, :], axis=3).astype(jnp.int32)
    order_scores = jax.random.randint(subkeys[5], (N_GROUP, N_DP, N_GROUP), 0, 1 << 20) * 8 + jnp.arange(N_GROUP)
    shuffle = jnp.argsort(order_scores, axis=-1, stable=True)
    return (reorder_table(sizes_raw, shuffle), reorder_table(groups_raw, shuffle), reorder_table(offsets_raw, shuffle))


def draw_image_rows(key, part):
    tables = plan_images(key)
    return tables[0]


def draw_image_group(key, part):
    tables = plan_images(key)
    return tables[1]


def draw_image_offset(key, part):
    tables = plan_images(key)
    return tables[2]


def shard_levels(rng, shape, cuts, least, largest):
    gain = 1.0
    for dim, shards_of in cuts:
        draws = jax.random.uniform(jax.random.fold_in(jax.random.fold_in(rng, 6), dim), (shards_of,), jnp.float32, least / len(cuts), largest / len(cuts))
        gain = gain * jnp.repeat(jnp.exp(draws), shape[dim] // shards_of).reshape((-1,) + (1,) * (len(shape) - 1 - dim))
    return gain


def normal_values(own_key, dims, width, bound, cuts=(), kind=jnp.bfloat16):
    entries = width * jax.random.normal(own_key, dims, jnp.float32)
    if cuts:
        entries = entries * shard_levels(own_key, dims, cuts, -0.22, 0.18)
    return jnp.clip(entries, -bound, bound).astype(kind)


def setup_inputs(seed: int = 0) -> dict:
    keys = jax.random.split(jax.random.key(seed), 8)
    return {
        "hidden": normal_values(keys[0], (VROWS, D), 1.0, 6.0, ((0, 8), (1, 4))),
        "out_weight": normal_values(keys[1], (D, D), D ** -0.5, 0.0625, ((0, 4), (1, 2))),
        "out_bias": normal_values(keys[2], (D,), 0.5, 3.0, ((0, 2),)),
        "text_embeds": normal_values(keys[3], (TOKENS, D), 1.0, 6.0, ((0, 16), (1, 2))),
        "image_rows": draw_image_rows(jax.random.fold_in(keys[7], 71), 0),
        "image_group": draw_image_group(jax.random.fold_in(keys[7], 71), 0),
        "image_offset": draw_image_offset(jax.random.fold_in(keys[7], 71), 0),
    }


def reference(hidden, out_weight, out_bias, text_embeds, image_rows, image_group, image_offset):
    block_width = D // N_DP

    def add_block(running, block_index):
        hidden_part = lax.dynamic_slice_in_dim(hidden, block_index * block_width, block_width, 1)
        weight_part = lax.dynamic_slice_in_dim(out_weight, block_index * block_width, block_width, 0)
        partial_sum = jnp.dot(hidden_part, weight_part, preferred_element_type=jnp.float32)
        rounded = lax.optimization_barrier(partial_sum.astype(jnp.bfloat16)).astype(jnp.float32)
        return running + rounded, None

    summed = lax.scan(add_block, jnp.zeros((VROWS, D), jnp.float32), jnp.arange(N_DP, dtype=jnp.int32))[0]
    projected = (summed + out_bias.astype(jnp.float32)[None, :]).astype(jnp.bfloat16)
    sources = N_GROUP * N_DP
    image_ends = jnp.cumsum(image_rows, axis=1).astype(jnp.int32)
    image_starts = (image_ends - image_rows).astype(jnp.int32)
    row_local = jnp.arange(ROW_DEV, dtype=jnp.int32)
    member = ((row_local[None, :, None] >= image_starts[:, None, :]) & (row_local[None, :, None] < image_ends[:, None, :])).astype(jnp.int32)
    target_group = jnp.sum(member * image_group[:, None, :], axis=2).astype(jnp.int32)
    first_row = jnp.sum(member * image_starts[:, None, :], axis=2).astype(jnp.int32)
    first_token = jnp.sum(member * image_offset[:, None, :], axis=2).astype(jnp.int32)
    replica = jnp.arange(sources, dtype=jnp.int32) % N_DP
    target = (target_group * N_DP + replica[:, None]) * TOK_DEV + first_token + row_local[None, :] - first_row
    return text_embeds.at[target.reshape(-1).astype(jnp.int32)].set(projected)
```

```python
import functools

import jax
import jax.numpy as jnp
from jax import lax
from jax.experimental import pallas as pl
from jax.experimental.pallas import tpu as pltpu
from jax.sharding import PartitionSpec as P

CAP = 64
MESH = pl.DeviceIdType.MESH
F32 = jnp.float32
BF16 = jnp.bfloat16


def project_kernel(
    n_group, n_dp, n_tensor, width, skew,
    rows_ref, group_ref, offset_ref, hidden_ref, weight_ref, bias_ref,
    incoming_ref, meta_ref,
    weight, rows, own, up_in, down_in, up_out, down_out, pick, parts, meta,
    weight_sem, rows_send, rows_recv, rows_local,
    up_send, up_recv, down_send, down_recv,
    part_send, part_recv, part_local, meta_send, meta_recv, meta_local,
):
    g, d, t = lax.axis_index("group"), lax.axis_index("dp"), lax.axis_index("tensor")
    blocks = weight.shape[0]
    rep = own.shape[2]
    device_rows = hidden_ref.shape[0]
    columns = lambda b: pl.ds(pl.multiple_of(b * width, width), width)
    above, below = (g, d + 1, t), (g, d - 1, t)

    def row_slot(s):
        return rows.at[pl.ds(pl.multiple_of(s * device_rows, device_rows), device_rows), :]

    own_rows = pltpu.make_async_copy(hidden_ref, row_slot(t), rows_local)
    own_rows.start()

    def load_weight(b):
        return pltpu.make_async_copy(weight_ref.at[:, columns(b)], weight.at[b], weight_sem.at[b])

    barrier = pltpu.get_barrier_semaphore()
    for i in range(1, n_tensor):
        pl.semaphore_signal(barrier, inc=1, device_id=(g, d, lax.rem(t + i, n_tensor)), device_id_type=MESH)
    for i in range(1, n_group):
        pl.semaphore_signal(barrier, inc=1, device_id=(lax.rem(g + i, n_group), d, t), device_id_type=MESH)

    @pl.when(d > 0)
    def _():
        pl.semaphore_signal(barrier, inc=1, device_id=below, device_id_type=MESH)

    @pl.when(d < n_dp - 1)
    def _():
        pl.semaphore_signal(barrier, inc=1, device_id=above, device_id_type=MESH)

    neighbours = lax.div(d + n_dp - 1, n_dp) + lax.div(2 * n_dp - 2 - d, n_dp)
    pl.semaphore_wait(barrier, n_tensor - 1 + n_group - 1 + neighbours)

    def send_rows(i):
        return pltpu.make_async_remote_copy(
            src_ref=hidden_ref, dst_ref=row_slot(t), send_sem=rows_send.at[i], recv_sem=rows_recv.at[i],
            device_id=(g, d, lax.rem(t + i, n_tensor)), device_id_type=MESH,
        )

    def receive_rows(i):
        return pltpu.make_async_remote_copy(
            src_ref=hidden_ref, dst_ref=row_slot(lax.rem(t + n_tensor - i, n_tensor)),
            send_sem=rows_send.at[i], recv_sem=rows_recv.at[i],
            device_id=(g, d, lax.rem(t + i, n_tensor)), device_id_type=MESH,
        )

    for i in range(1, n_tensor):
        send_rows(i).start()

    def start_weight(b, carry):
        load_weight(b).start()
        return carry

    lax.fori_loop(0, blocks, start_weight, 0)

    at_row = lax.broadcasted_iota(jnp.int32, (CAP, rep), 1)
    at_slot = lax.broadcasted_iota(jnp.int32, (CAP, rep), 0)
    line = lax.broadcasted_iota(jnp.int32, (8, 128), 0)
    for q in range(n_group):
        start, first, size, token = 0, 0, 0, 0
        for k in range(n_group):
            mine = group_ref[0, k] == q
            first = jnp.where(mine, start, first)
            size = jnp.where(mine, rows_ref[0, k], size)
            token = jnp.where(mine, offset_ref[0, k], token)
            start = start + rows_ref[0, k]
        hit = (at_row == at_slot + first) & (at_slot < size)
        pick[q * CAP:(q + 1) * CAP, :] = jnp.where(hit, 1.0, 0.0).astype(BF16)
        meta[q] = jnp.where(line == 0, token, size)

    def send_meta(i):
        q = lax.rem(g + i, n_group)
        return pltpu.make_async_remote_copy(
            src_ref=meta.at[q], dst_ref=meta_ref.at[g], send_sem=meta_send.at[i], recv_sem=meta_recv.at[i],
            device_id=(q, d, t), device_id_type=MESH,
        )

    def receive_meta(i):
        q = lax.rem(g + n_group - i, n_group)
        return pltpu.make_async_remote_copy(
            src_ref=meta.at[q], dst_ref=meta_ref.at[q], send_sem=meta_send.at[i], recv_sem=meta_recv.at[i],
            device_id=(q, d, t), device_id_type=MESH,
        )

    for i in range(1, n_group):
        send_meta(i).start()
    own_meta = pltpu.make_async_copy(meta.at[g], meta_ref.at[g], meta_local)
    own_meta.start()

    def upward(source, b, c):
        return pltpu.make_async_remote_copy(
            src_ref=source.at[b, c], dst_ref=up_in.at[b, c],
            send_sem=up_send.at[b * n_dp + c], recv_sem=up_recv.at[b * n_dp + c],
            device_id=above, device_id_type=MESH,
        )

    def downward(source, b, c):
        return pltpu.make_async_remote_copy(
            src_ref=source.at[b, c], dst_ref=down_in.at[b, c],
            send_sem=down_send.at[b * n_dp + c], recv_sem=down_recv.at[b * n_dp + c],
            device_id=below, device_id_type=MESH,
        )

    def send_part(b, i):
        q = lax.rem(g + i, n_group)
        return pltpu.make_async_remote_copy(
            src_ref=parts.at[b, q], dst_ref=incoming_ref.at[g, :, columns(b)],
            send_sem=part_send.at[b * n_group + i], recv_sem=part_recv.at[b * n_group + i],
            device_id=(q, d, t), device_id_type=MESH,
        )

    def receive_part(b, i):
        q = lax.rem(g + n_group - i, n_group)
        return pltpu.make_async_remote_copy(
            src_ref=parts.at[b, q], dst_ref=incoming_ref.at[q, :, columns(b)],
            send_sem=part_send.at[b * n_group + i], recv_sem=part_recv.at[b * n_group + i],
            device_id=(q, d, t), device_id_type=MESH,
        )

    def own_part(b):
        return pltpu.make_async_copy(parts.at[b, g], incoming_ref.at[g, :, columns(b)], part_local.at[b])

    own_rows.wait()
    for i in range(1, n_tensor):
        receive_rows(i).wait_recv()

    def multiply(b):
        load_weight(b).wait()
        product = jnp.dot(rows[...], weight[b], preferred_element_type=F32).astype(BF16)
        own[b] = product.reshape(n_dp, rep, width)

        @pl.when(d == 0)
        def _():
            def go(i, carry):
                upward(own, b, n_dp - 1 - i).start()
                return carry
            lax.fori_loop(0, n_dp - 1, go, 0)

        @pl.when(d == n_dp - 1)
        def _():
            def go(i, carry):
                downward(own, b, i).start()
                return carry
            lax.fori_loop(0, n_dp - 1, go, 0)

    def pass_up(b):
        @pl.when(d > 0)
        def _():
            def go(i, carry):
                c = n_dp - 1 - i
                upward(up_out, b, c).wait_recv()
                up_out[b, c] = (own[b, c].astype(F32) + up_in[b, c].astype(F32)).astype(BF16)
                upward(up_out, b, c).start()
                return carry
            lax.fori_loop(0, n_dp - 1 - d, go, 0)

    def pass_down(b):
        @pl.when(d < n_dp - 1)
        def _():
            def go(c, carry):
                downward(down_out, b, c).wait_recv()
                down_out[b, c] = (own[b, c].astype(F32) + down_in[b, c].astype(F32)).astype(BF16)
                downward(down_out, b, c).start()
                return carry
            lax.fori_loop(0, d, go, 0)

    def finish(b):
        @pl.when(d > 0)
        def _():
            upward(up_out, b, d).wait_recv()

        @pl.when(d < n_dp - 1)
        def _():
            downward(down_out, b, d).wait_recv()

        from_below = jnp.where(d > 0, up_in[b, d].astype(F32), 0.0)
        from_above = jnp.where(d < n_dp - 1, down_in[b, d].astype(F32), 0.0)
        total = own[b, d].astype(F32) + from_below + from_above + bias_ref[:, columns(b)].astype(F32)
        chosen = jnp.dot(pick[...], total.astype(BF16), preferred_element_type=F32).astype(BF16)
        parts[b] = chosen.reshape(n_group, CAP, width)
        for i in range(1, n_group):
            send_part(b, i).start()
        own_part(b).start()

    def step(s, carry):
        @pl.when(s < blocks)
        def _():
            multiply(s)

        @pl.when(s >= skew)
        def _():
            b = s - skew

            @pl.when(2 * d < n_dp)
            def _():
                pass_up(b)
                pass_down(b)

            @pl.when(2 * d >= n_dp)
            def _():
                pass_down(b)
                pass_up(b)

            finish(b)

        return carry

    lax.fori_loop(0, blocks + skew, step, 0)

    def drain(b, carry):
        def up(i, c2):
            upward(own, b, d + 1 + i).wait_send()
            return c2
        lax.fori_loop(0, n_dp - 1 - d, up, 0)

        def down(c, c2):
            downward(own, b, c).wait_send()
            return c2
        lax.fori_loop(0, d, down, 0)
        for i in range(1, n_group):
            send_part(b, i).wait_send()
            receive_part(b, i).wait_recv()
        own_part(b).wait()
        return carry

    for i in range(1, n_tensor):
        send_rows(i).wait_send()
    for i in range(1, n_group):
        send_meta(i).wait_send()
        receive_meta(i).wait_recv()
    own_meta.wait()
    lax.fori_loop(0, blocks, drain, 0)


def project(hidden, out_weight, out_bias, image_rows, image_group, image_offset):
    n_group, n_dp, n_tensor = lax.axis_size("group"), lax.axis_size("dp"), lax.axis_size("tensor")
    depth, cols = out_weight.shape
    all_rows = hidden.shape[0] * n_tensor
    rep = all_rows // n_dp
    width = min(512, cols)
    blocks = cols // width
    skew = min(2, blocks)
    dma = lambda count: pltpu.SemaphoreType.DMA((count,))
    moving = pltpu.VMEM((blocks, n_dp, rep, width), BF16)
    anywhere = pl.BlockSpec(memory_space=pl.ANY)
    scalars = pl.BlockSpec(memory_space=pltpu.SMEM)
    return pl.pallas_call(
        functools.partial(project_kernel, n_group, n_dp, n_tensor, width, skew),
        out_shape=(
            jax.ShapeDtypeStruct((n_group, CAP, cols), BF16),
            jax.ShapeDtypeStruct((n_group, 8, 128), jnp.int32),
        ),
        in_specs=[scalars, scalars, scalars, anywhere, anywhere, pl.BlockSpec(memory_space=pltpu.VMEM)],
        out_specs=(anywhere, anywhere),
        scratch_shapes=[
            pltpu.VMEM((blocks, depth, width), BF16),
            pltpu.VMEM((all_rows, depth), BF16),
            moving, moving, moving, moving, moving,
            pltpu.VMEM((n_group * CAP, rep), BF16),
            pltpu.VMEM((blocks, n_group, CAP, width), BF16),
            pltpu.VMEM((n_group, 8, 128), jnp.int32),
            dma(blocks), dma(n_tensor), dma(n_tensor), pltpu.SemaphoreType.DMA,
            dma(blocks * n_dp), dma(blocks * n_dp), dma(blocks * n_dp), dma(blocks * n_dp),
            dma(blocks * n_group), dma(blocks * n_group), dma(blocks),
            dma(n_group), dma(n_group), pltpu.SemaphoreType.DMA,
        ],
        compiler_params=pltpu.CompilerParams(
            collective_id=0, has_side_effects=True, vmem_limit_bytes=56 * 1024 * 1024
        ),
        cost_estimate=pl.CostEstimate(
            flops=2 * all_rows * depth * cols, bytes_accessed=2 * depth * cols, transcendentals=0
        ),
        name="project",
    )(image_rows, image_group, image_offset, hidden, out_weight, out_bias[None, :])


def per_device(hidden, out_weight, out_bias, text_embeds, image_rows, image_group, image_offset):
    incoming, meta = project(hidden, out_weight, out_bias, image_rows, image_group, image_offset)
    slot = lax.iota(jnp.int32, CAP)[None, :]
    token = jnp.where(slot < meta[:, 1, :1], meta[:, 0, :1] + slot, -1).reshape(-1)
    landing = token[None, :] == lax.iota(jnp.int32, text_embeds.shape[0])[:, None]
    placed = jnp.dot(
        landing.astype(BF16), incoming.reshape(-1, incoming.shape[2]), preferred_element_type=F32
    )
    visual = jnp.any(landing, axis=1)
    return jnp.where(visual[:, None], placed.astype(BF16), text_embeds)


def solution(mesh):
    return jax.shard_map(
        per_device,
        mesh=mesh,
        in_specs=(
            P(("group", "tensor"), "dp"),
            P("dp", "tensor"),
            P("tensor"),
            P(("group", "dp"), "tensor"),
            P(("group", "dp"), None),
            P(("group", "dp"), None),
            P(("group", "dp"), None),
        ),
        out_specs=P(("group", "dp"), "tensor"),
        check_vma=False,
    )
```

```python
import functools

import jax
import jax.numpy as jnp
from jax import lax
from jax.experimental import pallas as pl
from jax.experimental.pallas import tpu as pltpu
from jax.sharding import PartitionSpec as P

CAP = 64
WIDTH = 512
SKEW = 2
VMEM_MIB = 48
MESH = pl.DeviceIdType.MESH
F32 = jnp.float32
BF16 = jnp.bfloat16


def project_kernel(
    n_group, n_dp, n_tensor, width, skew,
    rows_ref, group_ref, offset_ref, hidden_ref, weight_ref, bias_ref, text_ref,
    embeds_ref,
    weight, rows, own, arrived, pick, parts, incoming, meta, meta_in, landing, visual, text,
    weight_sem, rows_send, rows_recv, rows_local,
    up_send, up_recv, down_send, down_recv,
    part_send, part_recv, meta_send, meta_recv, text_sem, embeds_sem,
):
    g, d, t = lax.axis_index("group"), lax.axis_index("dp"), lax.axis_index("tensor")
    blocks = weight.shape[0]
    rep = own.shape[2]
    device_rows = hidden_ref.shape[0]
    columns = lambda b: pl.ds(pl.multiple_of(b * width, width), width)
    above, below = (g, d + 1, t), (g, d - 1, t)

    def row_slot(s):
        return rows.at[pl.ds(pl.multiple_of(s * device_rows, device_rows), device_rows), :]

    own_rows = pltpu.make_async_copy(hidden_ref, row_slot(t), rows_local)
    own_rows.start()

    def load_weight(b):
        return pltpu.make_async_copy(weight_ref.at[:, columns(b)], weight.at[b], weight_sem.at[b])

    def load_text(b):
        return pltpu.make_async_copy(text_ref.at[:, columns(b)], text.at[b], text_sem.at[b])

    def store_embeds(b):
        return pltpu.make_async_copy(text.at[b], embeds_ref.at[:, columns(b)], embeds_sem.at[b])

    load_weight(0).start()

    barrier = pltpu.get_barrier_semaphore()
    for i in range(1, n_tensor):
        pl.semaphore_signal(barrier, inc=1, device_id=(g, d, lax.rem(t + i, n_tensor)), device_id_type=MESH)
    for i in range(1, n_group):
        pl.semaphore_signal(barrier, inc=1, device_id=(lax.rem(g + i, n_group), d, t), device_id_type=MESH)

    @pl.when(d > 0)
    def _():
        pl.semaphore_signal(barrier, inc=1, device_id=below, device_id_type=MESH)

    @pl.when(d < n_dp - 1)
    def _():
        pl.semaphore_signal(barrier, inc=1, device_id=above, device_id_type=MESH)

    neighbours = lax.div(d + n_dp - 1, n_dp) + lax.div(2 * n_dp - 2 - d, n_dp)
    pl.semaphore_wait(barrier, n_tensor - 1 + n_group - 1 + neighbours)

    def send_rows(i):
        return pltpu.make_async_remote_copy(
            src_ref=hidden_ref, dst_ref=row_slot(t), send_sem=rows_send.at[i], recv_sem=rows_recv.at[i],
            device_id=(g, d, lax.rem(t + i, n_tensor)), device_id_type=MESH,
        )

    def receive_rows(i):
        return pltpu.make_async_remote_copy(
            src_ref=hidden_ref, dst_ref=row_slot(lax.rem(t + n_tensor - i, n_tensor)),
            send_sem=rows_send.at[i], recv_sem=rows_recv.at[i],
            device_id=(g, d, lax.rem(t + i, n_tensor)), device_id_type=MESH,
        )

    for i in range(1, n_tensor):
        send_rows(i).start()


    def send_meta(i):
        q = lax.rem(g + i, n_group)
        return pltpu.make_async_remote_copy(
            src_ref=meta.at[q], dst_ref=meta_in.at[g], send_sem=meta_send.at[i], recv_sem=meta_recv.at[i],
            device_id=(q, d, t), device_id_type=MESH,
        )

    def receive_meta(i):
        q = lax.rem(g + n_group - i, n_group)
        return pltpu.make_async_remote_copy(
            src_ref=meta.at[q], dst_ref=meta_in.at[q], send_sem=meta_send.at[i], recv_sem=meta_recv.at[i],
            device_id=(q, d, t), device_id_type=MESH,
        )

    def plan_sends():
        at_row = lax.broadcasted_iota(jnp.int32, (CAP, rep), 1)
        at_slot = lax.broadcasted_iota(jnp.int32, (CAP, rep), 0)
        line = lax.broadcasted_iota(jnp.int32, (8, 128), 0)
        for q in range(n_group):
            start, first, size, token = 0, 0, 0, 0
            for k in range(n_group):
                mine = group_ref[0, k] == q
                first = jnp.where(mine, start, first)
                size = jnp.where(mine, rows_ref[0, k], size)
                token = jnp.where(mine, offset_ref[0, k], token)
                start = start + rows_ref[0, k]
            hit = (at_row == at_slot + first) & (at_slot < size)
            pick[q * CAP:(q + 1) * CAP, :] = jnp.where(hit, 1.0, 0.0).astype(BF16)
            meta[q] = jnp.where(line == 0, token, size)
        for i in range(1, n_group):
            send_meta(i).start()
        meta_in[g] = meta[g]

    def plan_landing():
        for i in range(1, n_group):
            receive_meta(i).wait_recv()
        shape = (landing.shape[0], 128)
        at_token = lax.broadcasted_iota(jnp.int32, shape, 0)
        lane = lax.broadcasted_iota(jnp.int32, shape, 1)
        seen = jnp.zeros(shape, jnp.int32)
        for tile in range(n_group * CAP // 128):
            hit = jnp.zeros(shape, jnp.int32)
            for q in range(n_group):
                token, size = meta_in[q, 0:1, :], meta_in[q, 1:2, :]
                slot = lane + (tile * 128 - q * CAP)
                inside = (slot >= 0) & (slot < size) & (at_token == token + slot)
                hit = jnp.where(inside, 1, hit)
            landing[:, tile * 128:(tile + 1) * 128] = hit.astype(F32).astype(BF16)
        for q in range(n_group):
            token, size = meta_in[q, 0:1, :], meta_in[q, 1:2, :]
            seen = jnp.where((at_token >= token) & (at_token < token + size), 1, seen)
        visual[...] = seen

    def upward(b, c):
        return pltpu.make_async_remote_copy(
            src_ref=own.at[b, c], dst_ref=arrived.at[b, c + 1],
            send_sem=up_send.at[b * n_dp + c], recv_sem=up_recv.at[b * n_dp + c],
            device_id=above, device_id_type=MESH,
        )

    def downward(b, c):
        return pltpu.make_async_remote_copy(
            src_ref=own.at[b, c], dst_ref=arrived.at[b, c],
            send_sem=down_send.at[b * n_dp + c], recv_sem=down_recv.at[b * n_dp + c],
            device_id=below, device_id_type=MESH,
        )

    def send_part(b, i):
        q = lax.rem(g + i, n_group)
        return pltpu.make_async_remote_copy(
            src_ref=parts.at[b, q], dst_ref=incoming.at[b, g],
            send_sem=part_send.at[b * n_group + i], recv_sem=part_recv.at[b * n_group + i],
            device_id=(q, d, t), device_id_type=MESH,
        )

    def receive_part(b, i):
        q = lax.rem(g + n_group - i, n_group)
        return pltpu.make_async_remote_copy(
            src_ref=parts.at[b, q], dst_ref=incoming.at[b, q],
            send_sem=part_send.at[b * n_group + i], recv_sem=part_recv.at[b * n_group + i],
            device_id=(q, d, t), device_id_type=MESH,
        )

    replicas = device_rows // rep

    def send_ends(b, low, high):
        @pl.when(d == 0)
        def _():
            def go(i, carry):
                c = high - 1 - i

                @pl.when(c > 0)
                def _():
                    upward(b, c).start()
                return carry
            lax.fori_loop(0, high - low, go, 0)

        @pl.when(d == n_dp - 1)
        def _():
            def go(c, carry):
                @pl.when(c < n_dp - 1)
                def _():
                    downward(b, c).start()
                return carry
            lax.fori_loop(low, high, go, 0)

    def multiply_part(slot):
        product = jnp.dot(row_slot(slot)[...], weight[0], preferred_element_type=F32).astype(BF16)
        own[0, pl.ds(slot * replicas, replicas)] = product.reshape(replicas, rep, width)
        send_ends(0, slot * replicas, (slot + 1) * replicas)

    def multiply(b):
        load_weight(b).wait()
        product = jnp.dot(rows[...], weight[b], preferred_element_type=F32).astype(BF16)
        own[b] = product.reshape(n_dp, rep, width)
        send_ends(b, 0, n_dp)

    own_rows.wait()
    load_weight(0).wait()
    multiply_part(t)

    def start_weight(b, carry):
        load_weight(b).start()
        return carry

    lax.fori_loop(1, blocks, start_weight, 0)

    def start_text(b, carry):
        load_text(b).start()
        return carry

    lax.fori_loop(0, blocks, start_text, 0)
    plan_sends()
    for i in range(1, n_tensor):
        receive_rows(i).wait_recv()
        multiply_part(lax.rem(t + n_tensor - i, n_tensor))

    def pass_up(b):
        @pl.when(d > 0)
        def _():
            def go(i, carry):
                c = n_dp - 1 - i
                upward(b, c).wait_recv()
                own[b, c] = (own[b, c].astype(F32) + arrived[b, c + 1].astype(F32)).astype(BF16)
                upward(b, c).start()
                return carry
            lax.fori_loop(0, n_dp - 1 - d, go, 0)

    def pass_down(b):
        @pl.when(d < n_dp - 1)
        def _():
            def go(c, carry):
                downward(b, c).wait_recv()
                own[b, c] = (own[b, c].astype(F32) + arrived[b, c].astype(F32)).astype(BF16)
                downward(b, c).start()
                return carry
            lax.fori_loop(0, d, go, 0)

    def finish(b):
        @pl.when(d > 0)
        def _():
            upward(b, d).wait_recv()

        @pl.when(d < n_dp - 1)
        def _():
            downward(b, d).wait_recv()

        from_below = jnp.where(d > 0, arrived[b, d + 1].astype(F32), 0.0)
        from_above = jnp.where(d < n_dp - 1, arrived[b, d].astype(F32), 0.0)
        total = own[b, d].astype(F32) + from_below + from_above + bias_ref[columns(b)].astype(F32).reshape(1, width)
        chosen = jnp.dot(pick[...], total.astype(BF16), preferred_element_type=F32).astype(BF16)
        parts[b] = chosen.reshape(n_group, CAP, width)
        for i in range(1, n_group):
            send_part(b, i).start()
        incoming[b, g] = parts[b, g]

    def place(b):
        for i in range(1, n_group):
            receive_part(b, i).wait_recv()
        load_text(b).wait()
        block = incoming[b].reshape(n_group * CAP, width)
        placed = jnp.dot(landing[...], block, preferred_element_type=F32)
        keep = visual[...] == 0
        for k in range(0, width, 128):
            words = text[b, :, k:k + 128].astype(F32)
            text[b, :, k:k + 128] = jnp.where(keep, words, placed[:, k:k + 128]).astype(BF16)
        store_embeds(b).start()

    def step(s, carry):
        @pl.when(s < blocks)
        def _():
            multiply(s)

        @pl.when((s >= skew) & (s < blocks + skew))
        def _():
            b = s - skew

            @pl.when(2 * d < n_dp)
            def _():
                pass_up(b)
                pass_down(b)

            @pl.when(2 * d >= n_dp)
            def _():
                pass_down(b)
                pass_up(b)

            finish(b)

        @pl.when(s == skew)
        def _():
            plan_landing()

        @pl.when(s > skew)
        def _():
            place(s - skew - 1)

        return carry

    lax.fori_loop(1, blocks + skew + 1, step, 0)

    def drain(b, carry):
        def up(i, c2):
            upward(b, d + 1 + i).wait_send()
            return c2
        lax.fori_loop(0, n_dp - 1 - d, up, 0)

        def down(c, c2):
            downward(b, c).wait_send()
            return c2
        lax.fori_loop(0, d, down, 0)
        for i in range(1, n_group):
            send_part(b, i).wait_send()
        store_embeds(b).wait()
        return carry

    for i in range(1, n_tensor):
        send_rows(i).wait_send()
    for i in range(1, n_group):
        send_meta(i).wait_send()
    lax.fori_loop(0, blocks, drain, 0)


def per_device(hidden, out_weight, out_bias, text_embeds, image_rows, image_group, image_offset):
    n_group, n_dp, n_tensor = lax.axis_size("group"), lax.axis_size("dp"), lax.axis_size("tensor")
    depth, cols = out_weight.shape
    tokens = text_embeds.shape[0]
    all_rows = hidden.shape[0] * n_tensor
    rep = all_rows // n_dp
    width = min(WIDTH, cols)
    blocks = cols // width
    skew = min(SKEW, blocks)
    dma = lambda count: pltpu.SemaphoreType.DMA((count,))
    anywhere = pl.BlockSpec(memory_space=pl.ANY)
    scalars = pl.BlockSpec(memory_space=pltpu.SMEM)
    return pl.pallas_call(
        functools.partial(project_kernel, n_group, n_dp, n_tensor, width, skew),
        out_shape=jax.ShapeDtypeStruct(text_embeds.shape, BF16),
        in_specs=[
            scalars, scalars, scalars, anywhere, anywhere, pl.BlockSpec(memory_space=pltpu.VMEM), anywhere,
        ],
        out_specs=anywhere,
        scratch_shapes=[
            pltpu.VMEM((blocks, depth, width), BF16),
            pltpu.VMEM((all_rows, depth), BF16),
            pltpu.VMEM((blocks, n_dp, rep, width), BF16),
            pltpu.VMEM((blocks, n_dp + 1, rep, width), BF16),
            pltpu.VMEM((n_group * CAP, rep), BF16),
            pltpu.VMEM((blocks, n_group, CAP, width), BF16),
            pltpu.VMEM((blocks, n_group, CAP, width), BF16),
            pltpu.VMEM((n_group, 8, 128), jnp.int32),
            pltpu.VMEM((n_group, 8, 128), jnp.int32),
            pltpu.VMEM((tokens, n_group * CAP), BF16),
            pltpu.VMEM((tokens, 128), jnp.int32),
            pltpu.VMEM((blocks, tokens, width), BF16),
            dma(blocks), dma(n_tensor), dma(n_tensor), pltpu.SemaphoreType.DMA,
            dma(blocks * n_dp), dma(blocks * n_dp), dma(blocks * n_dp), dma(blocks * n_dp),
            dma(blocks * n_group), dma(blocks * n_group), dma(n_group), dma(n_group),
            dma(blocks), dma(blocks),
        ],
        compiler_params=pltpu.CompilerParams(
            collective_id=0, has_side_effects=True, vmem_limit_bytes=VMEM_MIB * 1024 * 1024
        ),
        cost_estimate=pl.CostEstimate(
            flops=2 * all_rows * depth * cols, bytes_accessed=2 * depth * cols, transcendentals=0
        ),
        name="project",
    )(image_rows, image_group, image_offset, hidden, out_weight, out_bias, text_embeds)


def solution(mesh):
    return jax.shard_map(
        per_device,
        mesh=mesh,
        in_specs=(
            P(("group", "tensor"), "dp"),
            P("dp", "tensor"),
            P("tensor"),
            P(("group", "dp"), "tensor"),
            P(("group", "dp"), None),
            P(("group", "dp"), None),
            P(("group", "dp"), None),
        ),
        out_specs=P(("group", "dp"), "tensor"),
        check_vma=False,
    )
```

```python
import functools

import jax
import jax.numpy as jnp
from jax import lax
from jax.experimental import pallas as pl
from jax.experimental.pallas import tpu as pltpu
from jax.sharding import PartitionSpec as P

CAP = 64
WIDTH = 512
SKEW = 2
VMEM_MIB = 56
MESH = pl.DeviceIdType.MESH
F32 = jnp.float32
BF16 = jnp.bfloat16


def project_kernel(
    n_group, n_dp, n_tensor, width, skew,
    rows_hbm, group_hbm, offset_hbm, hidden_ref, weight_ref, bias_hbm, text_ref,
    embeds_ref,
    rows_ref, group_ref, offset_ref, bias_ref,
    weight, rows, own, arrived, pick, parts, incoming, meta, meta_in, landing, visual,
    small_sem, weight_sem, rows_send, rows_recv, rows_local,
    up_send, up_recv, down_send, down_recv,
    part_send, part_recv, meta_send, meta_recv, text_sem,
):
    g, d, t = lax.axis_index("group"), lax.axis_index("dp"), lax.axis_index("tensor")
    blocks = weight.shape[0]
    rep = own.shape[2]
    device_rows = hidden_ref.shape[0]
    columns = lambda b: pl.ds(pl.multiple_of(b * width, width), width)
    above, below = (g, d + 1, t), (g, d - 1, t)

    def row_slot(s):
        return rows.at[pl.ds(pl.multiple_of(s * device_rows, device_rows), device_rows), :]

    own_rows = pltpu.make_async_copy(hidden_ref, row_slot(t), rows_local)
    own_rows.start()

    def load_weight(b):
        return pltpu.make_async_copy(weight_ref.at[:, columns(b)], weight.at[b], weight_sem.at[b])

    def load_text(b):
        return pltpu.make_async_copy(text_ref.at[:, columns(b)], embeds_ref.at[:, columns(b)], text_sem.at[b])

    small = [
        pltpu.make_async_copy(source, target, small_sem.at[i])
        for i, (source, target) in enumerate((
            (rows_hbm, rows_ref), (group_hbm, group_ref), (offset_hbm, offset_ref), (bias_hbm, bias_ref),
        ))
    ]
    for copy in small:
        copy.start()
    load_weight(0).start()

    barrier = pltpu.get_barrier_semaphore()
    for i in range(1, n_tensor):
        pl.semaphore_signal(barrier, inc=1, device_id=(g, d, lax.rem(t + i, n_tensor)), device_id_type=MESH)
    for i in range(1, n_group):
        pl.semaphore_signal(barrier, inc=1, device_id=(lax.rem(g + i, n_group), d, t), device_id_type=MESH)

    @pl.when(d > 0)
    def _():
        pl.semaphore_signal(barrier, inc=1, device_id=below, device_id_type=MESH)

    @pl.when(d < n_dp - 1)
    def _():
        pl.semaphore_signal(barrier, inc=1, device_id=above, device_id_type=MESH)

    neighbours = lax.div(d + n_dp - 1, n_dp) + lax.div(2 * n_dp - 2 - d, n_dp)
    pl.semaphore_wait(barrier, n_tensor - 1 + n_group - 1 + neighbours)

    def send_rows(i):
        return pltpu.make_async_remote_copy(
            src_ref=hidden_ref, dst_ref=row_slot(t), send_sem=rows_send.at[i], recv_sem=rows_recv.at[i],
            device_id=(g, d, lax.rem(t + i, n_tensor)), device_id_type=MESH,
        )

    def receive_rows(i):
        return pltpu.make_async_remote_copy(
            src_ref=hidden_ref, dst_ref=row_slot(lax.rem(t + n_tensor - i, n_tensor)),
            send_sem=rows_send.at[i], recv_sem=rows_recv.at[i],
            device_id=(g, d, lax.rem(t + i, n_tensor)), device_id_type=MESH,
        )

    for i in range(1, n_tensor):
        send_rows(i).start()


    def send_meta(i):
        q = lax.rem(g + i, n_group)
        return pltpu.make_async_remote_copy(
            src_ref=meta.at[q], dst_ref=meta_in.at[g], send_sem=meta_send.at[i], recv_sem=meta_recv.at[i],
            device_id=(q, d, t), device_id_type=MESH,
        )

    def receive_meta(i):
        q = lax.rem(g + n_group - i, n_group)
        return pltpu.make_async_remote_copy(
            src_ref=meta.at[q], dst_ref=meta_in.at[q], send_sem=meta_send.at[i], recv_sem=meta_recv.at[i],
            device_id=(q, d, t), device_id_type=MESH,
        )

    def plan_sends():
        at_row = lax.broadcasted_iota(jnp.int32, (CAP, rep), 1)
        at_slot = lax.broadcasted_iota(jnp.int32, (CAP, rep), 0)
        line = lax.broadcasted_iota(jnp.int32, (8, 128), 0)
        for q in range(n_group):
            start, first, size, token = 0, 0, 0, 0
            for k in range(n_group):
                mine = group_ref[0, k] == q
                first = jnp.where(mine, start, first)
                size = jnp.where(mine, rows_ref[0, k], size)
                token = jnp.where(mine, offset_ref[0, k], token)
                start = start + rows_ref[0, k]
            hit = (at_row == at_slot + first) & (at_slot < size)
            pick[q * CAP:(q + 1) * CAP, :] = jnp.where(hit, 1.0, 0.0).astype(BF16)
            meta[q] = jnp.where(line == 0, token, size)
        for i in range(1, n_group):
            send_meta(i).start()
        meta_in[g] = meta[g]

    def plan_landing():
        for i in range(1, n_group):
            receive_meta(i).wait_recv()
        shape = (landing.shape[0], 128)
        at_token = lax.broadcasted_iota(jnp.int32, shape, 0)
        lane = lax.broadcasted_iota(jnp.int32, shape, 1)
        seen = jnp.zeros(shape, jnp.int32)
        for tile in range(n_group * CAP // 128):
            hit = jnp.zeros(shape, jnp.int32)
            for q in range(n_group):
                token, size = meta_in[q, 0:1, :], meta_in[q, 1:2, :]
                slot = lane + (tile * 128 - q * CAP)
                inside = (slot >= 0) & (slot < size) & (at_token == token + slot)
                hit = jnp.where(inside, 1, hit)
            landing[:, tile * 128:(tile + 1) * 128] = hit.astype(F32).astype(BF16)
        for q in range(n_group):
            token, size = meta_in[q, 0:1, :], meta_in[q, 1:2, :]
            seen = jnp.where((at_token >= token) & (at_token < token + size), 1, seen)
        visual[...] = seen

    def upward(b, c):
        return pltpu.make_async_remote_copy(
            src_ref=own.at[b, c], dst_ref=arrived.at[b, c + 1],
            send_sem=up_send.at[b * n_dp + c], recv_sem=up_recv.at[b * n_dp + c],
            device_id=above, device_id_type=MESH,
        )

    def downward(b, c):
        return pltpu.make_async_remote_copy(
            src_ref=own.at[b, c], dst_ref=arrived.at[b, c],
            send_sem=down_send.at[b * n_dp + c], recv_sem=down_recv.at[b * n_dp + c],
            device_id=below, device_id_type=MESH,
        )

    def send_part(b, i):
        q = lax.rem(g + i, n_group)
        return pltpu.make_async_remote_copy(
            src_ref=parts.at[b, q], dst_ref=incoming.at[b, g],
            send_sem=part_send.at[b * n_group + i], recv_sem=part_recv.at[b * n_group + i],
            device_id=(q, d, t), device_id_type=MESH,
        )

    def receive_part(b, i):
        q = lax.rem(g + n_group - i, n_group)
        return pltpu.make_async_remote_copy(
            src_ref=parts.at[b, q], dst_ref=incoming.at[b, q],
            send_sem=part_send.at[b * n_group + i], recv_sem=part_recv.at[b * n_group + i],
            device_id=(q, d, t), device_id_type=MESH,
        )

    replicas = device_rows // rep

    def send_ends(b, low, high):
        @pl.when(d == 0)
        def _():
            def go(i, carry):
                c = high - 1 - i

                @pl.when(c > 0)
                def _():
                    upward(b, c).start()
                return carry
            lax.fori_loop(0, high - low, go, 0)

        @pl.when(d == n_dp - 1)
        def _():
            def go(c, carry):
                @pl.when(c < n_dp - 1)
                def _():
                    downward(b, c).start()
                return carry
            lax.fori_loop(low, high, go, 0)

    def multiply_part(slot):
        product = jnp.dot(row_slot(slot)[...], weight[0], preferred_element_type=F32).astype(BF16)
        own[0, pl.ds(slot * replicas, replicas)] = product.reshape(replicas, rep, width)
        send_ends(0, slot * replicas, (slot + 1) * replicas)

    def multiply(b):
        load_weight(b).wait()
        product = jnp.dot(rows[...], weight[b], preferred_element_type=F32).astype(BF16)
        own[b] = product.reshape(n_dp, rep, width)
        send_ends(b, 0, n_dp)

    own_rows.wait()
    load_weight(0).wait()
    multiply_part(t)

    def start_weight(b, carry):
        load_weight(b).start()
        return carry

    lax.fori_loop(1, blocks, start_weight, 0)

    def start_text(b, carry):
        load_text(b).start()
        return carry

    lax.fori_loop(0, blocks, start_text, 0)
    for copy in small:
        copy.wait()
    plan_sends()
    for i in range(1, n_tensor):
        receive_rows(i).wait_recv()
        multiply_part(lax.rem(t + n_tensor - i, n_tensor))

    def pass_up(b):
        @pl.when(d > 0)
        def _():
            def go(i, carry):
                c = n_dp - 1 - i
                upward(b, c).wait_recv()
                own[b, c] = (own[b, c].astype(F32) + arrived[b, c + 1].astype(F32)).astype(BF16)
                upward(b, c).start()
                return carry
            lax.fori_loop(0, n_dp - 1 - d, go, 0)

    def pass_down(b):
        @pl.when(d < n_dp - 1)
        def _():
            def go(c, carry):
                downward(b, c).wait_recv()
                own[b, c] = (own[b, c].astype(F32) + arrived[b, c].astype(F32)).astype(BF16)
                downward(b, c).start()
                return carry
            lax.fori_loop(0, d, go, 0)

    def finish(b):
        @pl.when(d > 0)
        def _():
            upward(b, d).wait_recv()

        @pl.when(d < n_dp - 1)
        def _():
            downward(b, d).wait_recv()

        from_below = jnp.where(d > 0, arrived[b, d + 1].astype(F32), 0.0)
        from_above = jnp.where(d < n_dp - 1, arrived[b, d].astype(F32), 0.0)
        total = own[b, d].astype(F32) + from_below + from_above + bias_ref[columns(b)].astype(F32).reshape(1, width)
        chosen = jnp.dot(pick[...], total.astype(BF16), preferred_element_type=F32).astype(BF16)
        parts[b] = chosen.reshape(n_group, CAP, width)
        for i in range(1, n_group):
            send_part(b, i).start()
        incoming[b, g] = parts[b, g]

    def place(b):
        for i in range(1, n_group):
            receive_part(b, i).wait_recv()
        load_text(b).wait()
        block = incoming[b].reshape(n_group * CAP, width)
        placed = jnp.dot(landing[...], block, preferred_element_type=F32)
        keep = visual[...] == 0
        for k in range(0, width, 128):
            lanes = pl.ds(pl.multiple_of(b * width + k, 128), 128)
            words = embeds_ref[:, lanes].astype(F32)
            embeds_ref[:, lanes] = jnp.where(keep, words, placed[:, k:k + 128]).astype(BF16)

    def step(s, carry):
        @pl.when(s < blocks)
        def _():
            multiply(s)

        @pl.when((s >= skew) & (s < blocks + skew))
        def _():
            b = s - skew

            @pl.when(2 * d < n_dp)
            def _():
                pass_up(b)
                pass_down(b)

            @pl.when(2 * d >= n_dp)
            def _():
                pass_down(b)
                pass_up(b)

            finish(b)

        @pl.when(s == skew)
        def _():
            plan_landing()

        @pl.when(s > skew)
        def _():
            place(s - skew - 1)

        return carry

    lax.fori_loop(1, blocks + skew + 1, step, 0)

    def drain(b, carry):
        def up(i, c2):
            upward(b, d + 1 + i).wait_send()
            return c2
        lax.fori_loop(0, n_dp - 1 - d, up, 0)

        def down(c, c2):
            downward(b, c).wait_send()
            return c2
        lax.fori_loop(0, d, down, 0)
        for i in range(1, n_group):
            send_part(b, i).wait_send()
        return carry

    for i in range(1, n_tensor):
        send_rows(i).wait_send()
    for i in range(1, n_group):
        send_meta(i).wait_send()
    lax.fori_loop(0, blocks, drain, 0)


def per_device(hidden, out_weight, out_bias, text_embeds, image_rows, image_group, image_offset):
    n_group, n_dp, n_tensor = lax.axis_size("group"), lax.axis_size("dp"), lax.axis_size("tensor")
    depth, cols = out_weight.shape
    tokens = text_embeds.shape[0]
    all_rows = hidden.shape[0] * n_tensor
    rep = all_rows // n_dp
    width = min(WIDTH, cols)
    blocks = cols // width
    skew = min(SKEW, blocks)
    dma = lambda count: pltpu.SemaphoreType.DMA((count,))
    return pl.pallas_call(
        functools.partial(project_kernel, n_group, n_dp, n_tensor, width, skew),
        out_shape=pltpu.VMEM(text_embeds.shape, BF16),
        in_specs=[pl.BlockSpec(memory_space=pltpu.HBM)] * 7,
        out_specs=pl.BlockSpec(memory_space=pltpu.VMEM),
        scratch_shapes=[
            pltpu.SMEM(image_rows.shape, jnp.int32),
            pltpu.SMEM(image_group.shape, jnp.int32),
            pltpu.SMEM(image_offset.shape, jnp.int32),
            pltpu.VMEM(out_bias.shape, BF16),
            pltpu.VMEM((blocks, depth, width), BF16),
            pltpu.VMEM((all_rows, depth), BF16),
            pltpu.VMEM((blocks, n_dp, rep, width), BF16),
            pltpu.VMEM((blocks, n_dp + 1, rep, width), BF16),
            pltpu.VMEM((n_group * CAP, rep), BF16),
            pltpu.VMEM((blocks, n_group, CAP, width), BF16),
            pltpu.VMEM((blocks, n_group, CAP, width), BF16),
            pltpu.VMEM((n_group, 8, 128), jnp.int32),
            pltpu.VMEM((n_group, 8, 128), jnp.int32),
            pltpu.VMEM((tokens, n_group * CAP), BF16),
            pltpu.VMEM((tokens, 128), jnp.int32),
            dma(4), dma(blocks), dma(n_tensor), dma(n_tensor), pltpu.SemaphoreType.DMA,
            dma(blocks * n_dp), dma(blocks * n_dp), dma(blocks * n_dp), dma(blocks * n_dp),
            dma(blocks * n_group), dma(blocks * n_group), dma(n_group), dma(n_group),
            dma(blocks),
        ],
        compiler_params=pltpu.CompilerParams(
            collective_id=0, has_side_effects=True, vmem_limit_bytes=VMEM_MIB * 1024 * 1024
        ),
        cost_estimate=pl.CostEstimate(
            flops=2 * all_rows * depth * cols, bytes_accessed=2 * depth * cols, transcendentals=0
        ),
        name="project",
    )(image_rows, image_group, image_offset, hidden, out_weight, out_bias, text_embeds)


def solution(mesh):
    return jax.shard_map(
        per_device,
        mesh=mesh,
        in_specs=(
            P(("group", "tensor"), "dp"),
            P("dp", "tensor"),
            P("tensor"),
            P(("group", "dp"), "tensor"),
            P(("group", "dp"), None),
            P(("group", "dp"), None),
            P(("group", "dp"), None),
        ),
        out_specs=P(("group", "dp"), "tensor"),
        check_vma=False,
    )
```

```python
import functools

import jax
import jax.numpy as jnp
from jax import lax
from jax.experimental import pallas as pl
from jax.experimental.pallas import tpu as pltpu
from jax.sharding import PartitionSpec as P

CAP = 64
WIDTH = 1024
SKEW = 1
VMEM_MIB = 56
MESH = pl.DeviceIdType.MESH
F32 = jnp.float32
BF16 = jnp.bfloat16


def project_kernel(
    n_group, n_dp, n_tensor, width, skew,
    rows_hbm, group_hbm, offset_hbm, hidden_ref, weight_ref, bias_hbm, text_ref,
    embeds_ref,
    rows_ref, group_ref, offset_ref, bias_ref,
    weight, rows, own, arrived, pick, parts, incoming, meta, meta_in, landing, visual,
    small_sem, weight_sem, rows_send, rows_recv, rows_local,
    up_send, up_recv, down_send, down_recv,
    part_send, part_recv, meta_send, meta_recv, text_sem,
):
    g, d, t = lax.axis_index("group"), lax.axis_index("dp"), lax.axis_index("tensor")
    blocks = weight.shape[0]
    rep = own.shape[2]
    device_rows = hidden_ref.shape[0]
    columns = lambda b: pl.ds(pl.multiple_of(b * width, width), width)
    above, below = (g, d + 1, t), (g, d - 1, t)

    def row_slot(s):
        return rows.at[pl.ds(pl.multiple_of(s * device_rows, device_rows), device_rows), :]

    own_rows = pltpu.make_async_copy(hidden_ref, row_slot(t), rows_local)
    own_rows.start()

    def load_weight(b):
        return pltpu.make_async_copy(weight_ref.at[:, columns(b)], weight.at[b], weight_sem.at[b])

    def load_text(b):
        return pltpu.make_async_copy(text_ref.at[:, columns(b)], embeds_ref.at[:, columns(b)], text_sem.at[b])

    small = [
        pltpu.make_async_copy(source, target, small_sem.at[i])
        for i, (source, target) in enumerate((
            (rows_hbm, rows_ref), (group_hbm, group_ref), (offset_hbm, offset_ref), (bias_hbm, bias_ref),
        ))
    ]
    for copy in small:
        copy.start()
    load_weight(0).start()

    barrier = pltpu.get_barrier_semaphore()
    for i in range(1, n_tensor):
        pl.semaphore_signal(barrier, inc=1, device_id=(g, d, lax.rem(t + i, n_tensor)), device_id_type=MESH)
    for i in range(1, n_group):
        pl.semaphore_signal(barrier, inc=1, device_id=(lax.rem(g + i, n_group), d, t), device_id_type=MESH)

    @pl.when(d > 0)
    def _():
        pl.semaphore_signal(barrier, inc=1, device_id=below, device_id_type=MESH)

    @pl.when(d < n_dp - 1)
    def _():
        pl.semaphore_signal(barrier, inc=1, device_id=above, device_id_type=MESH)

    neighbours = lax.div(d + n_dp - 1, n_dp) + lax.div(2 * n_dp - 2 - d, n_dp)
    pl.semaphore_wait(barrier, n_tensor - 1 + n_group - 1 + neighbours)

    def send_rows(i):
        return pltpu.make_async_remote_copy(
            src_ref=hidden_ref, dst_ref=row_slot(t), send_sem=rows_send.at[i], recv_sem=rows_recv.at[i],
            device_id=(g, d, lax.rem(t + i, n_tensor)), device_id_type=MESH,
        )

    def receive_rows(i):
        return pltpu.make_async_remote_copy(
            src_ref=hidden_ref, dst_ref=row_slot(lax.rem(t + n_tensor - i, n_tensor)),
            send_sem=rows_send.at[i], recv_sem=rows_recv.at[i],
            device_id=(g, d, lax.rem(t + i, n_tensor)), device_id_type=MESH,
        )

    for i in range(1, n_tensor):
        send_rows(i).start()


    def send_meta(i):
        q = lax.rem(g + i, n_group)
        return pltpu.make_async_remote_copy(
            src_ref=meta.at[q], dst_ref=meta_in.at[g], send_sem=meta_send.at[i], recv_sem=meta_recv.at[i],
            device_id=(q, d, t), device_id_type=MESH,
        )

    def receive_meta(i):
        q = lax.rem(g + n_group - i, n_group)
        return pltpu.make_async_remote_copy(
            src_ref=meta.at[q], dst_ref=meta_in.at[q], send_sem=meta_send.at[i], recv_sem=meta_recv.at[i],
            device_id=(q, d, t), device_id_type=MESH,
        )

    def plan_sends():
        at_row = lax.broadcasted_iota(jnp.int32, (CAP, rep), 1)
        at_slot = lax.broadcasted_iota(jnp.int32, (CAP, rep), 0)
        line = lax.broadcasted_iota(jnp.int32, (8, 128), 0)
        for q in range(n_group):
            start, first, size, token = 0, 0, 0, 0
            for k in range(n_group):
                mine = group_ref[0, k] == q
                first = jnp.where(mine, start, first)
                size = jnp.where(mine, rows_ref[0, k], size)
                token = jnp.where(mine, offset_ref[0, k], token)
                start = start + rows_ref[0, k]
            hit = (at_row == at_slot + first) & (at_slot < size)
            pick[q * CAP:(q + 1) * CAP, :] = jnp.where(hit, 1.0, 0.0).astype(BF16)
            meta[q] = jnp.where(line == 0, token, size)
        for i in range(1, n_group):
            send_meta(i).start()
        meta_in[g] = meta[g]

    def plan_landing():
        for i in range(1, n_group):
            receive_meta(i).wait_recv()
        shape = (landing.shape[0], 128)
        at_token = lax.broadcasted_iota(jnp.int32, shape, 0)
        lane = lax.broadcasted_iota(jnp.int32, shape, 1)
        seen = jnp.zeros(shape, jnp.int32)
        for tile in range(n_group * CAP // 128):
            hit = jnp.zeros(shape, jnp.int32)
            for q in range(n_group):
                token, size = meta_in[q, 0:1, :], meta_in[q, 1:2, :]
                slot = lane + (tile * 128 - q * CAP)
                inside = (slot >= 0) & (slot < size) & (at_token == token + slot)
                hit = jnp.where(inside, 1, hit)
            landing[:, tile * 128:(tile + 1) * 128] = hit.astype(F32).astype(BF16)
        for q in range(n_group):
            token, size = meta_in[q, 0:1, :], meta_in[q, 1:2, :]
            seen = jnp.where((at_token >= token) & (at_token < token + size), 1, seen)
        visual[...] = seen

    def upward(b, c):
        return pltpu.make_async_remote_copy(
            src_ref=own.at[b, c], dst_ref=arrived.at[b, c + 1],
            send_sem=up_send.at[b * n_dp + c], recv_sem=up_recv.at[b * n_dp + c],
            device_id=above, device_id_type=MESH,
        )

    def downward(b, c):
        return pltpu.make_async_remote_copy(
            src_ref=own.at[b, c], dst_ref=arrived.at[b, c],
            send_sem=down_send.at[b * n_dp + c], recv_sem=down_recv.at[b * n_dp + c],
            device_id=below, device_id_type=MESH,
        )

    def send_part(b, i):
        q = lax.rem(g + i, n_group)
        return pltpu.make_async_remote_copy(
            src_ref=parts.at[b, q], dst_ref=incoming.at[b, g],
            send_sem=part_send.at[b * n_group + i], recv_sem=part_recv.at[b * n_group + i],
            device_id=(q, d, t), device_id_type=MESH,
        )

    def receive_part(b, i):
        q = lax.rem(g + n_group - i, n_group)
        return pltpu.make_async_remote_copy(
            src_ref=parts.at[b, q], dst_ref=incoming.at[b, q],
            send_sem=part_send.at[b * n_group + i], recv_sem=part_recv.at[b * n_group + i],
            device_id=(q, d, t), device_id_type=MESH,
        )

    replicas = device_rows // rep

    def send_ends(b, low, high):
        @pl.when(d == 0)
        def _():
            def go(i, carry):
                c = high - 1 - i

                @pl.when(c > 0)
                def _():
                    upward(b, c).start()
                return carry
            lax.fori_loop(0, high - low, go, 0)

        @pl.when(d == n_dp - 1)
        def _():
            def go(c, carry):
                @pl.when(c < n_dp - 1)
                def _():
                    downward(b, c).start()
                return carry
            lax.fori_loop(low, high, go, 0)

    def multiply_part(slot):
        product = jnp.dot(row_slot(slot)[...], weight[0], preferred_element_type=F32).astype(BF16)
        own[0, pl.ds(slot * replicas, replicas)] = product.reshape(replicas, rep, width)
        send_ends(0, slot * replicas, (slot + 1) * replicas)

    def multiply(b):
        load_weight(b).wait()
        product = jnp.dot(rows[...], weight[b], preferred_element_type=F32).astype(BF16)
        own[b] = product.reshape(n_dp, rep, width)
        send_ends(b, 0, n_dp)

    own_rows.wait()
    load_weight(0).wait()
    multiply_part(t)

    def start_weight(b, carry):
        load_weight(b).start()
        return carry

    lax.fori_loop(1, blocks, start_weight, 0)

    def start_text(b, carry):
        load_text(b).start()
        return carry

    lax.fori_loop(0, blocks, start_text, 0)
    for copy in small:
        copy.wait()
    plan_sends()
    for i in range(1, n_tensor):
        receive_rows(i).wait_recv()
        multiply_part(lax.rem(t + n_tensor - i, n_tensor))

    def pass_up(b):
        @pl.when(d > 0)
        def _():
            def go(i, carry):
                c = n_dp - 1 - i
                upward(b, c).wait_recv()
                own[b, c] = (own[b, c].astype(F32) + arrived[b, c + 1].astype(F32)).astype(BF16)
                upward(b, c).start()
                return carry
            lax.fori_loop(0, n_dp - 1 - d, go, 0)

    def pass_down(b):
        @pl.when(d < n_dp - 1)
        def _():
            def go(c, carry):
                downward(b, c).wait_recv()
                own[b, c] = (own[b, c].astype(F32) + arrived[b, c].astype(F32)).astype(BF16)
                downward(b, c).start()
                return carry
            lax.fori_loop(0, d, go, 0)

    def finish(b):
        @pl.when(d > 0)
        def _():
            upward(b, d).wait_recv()

        @pl.when(d < n_dp - 1)
        def _():
            downward(b, d).wait_recv()

        from_below = jnp.where(d > 0, arrived[b, d + 1].astype(F32), 0.0)
        from_above = jnp.where(d < n_dp - 1, arrived[b, d].astype(F32), 0.0)
        total = own[b, d].astype(F32) + from_below + from_above + bias_ref[columns(b)].astype(F32).reshape(1, width)
        chosen = jnp.dot(pick[...], total.astype(BF16), preferred_element_type=F32).astype(BF16)
        parts[b] = chosen.reshape(n_group, CAP, width)
        for i in range(1, n_group):
            send_part(b, i).start()
        incoming[b, g] = parts[b, g]

    def place(b):
        for i in range(1, n_group):
            receive_part(b, i).wait_recv()
        load_text(b).wait()
        block = incoming[b].reshape(n_group * CAP, width)
        placed = jnp.dot(landing[...], block, preferred_element_type=F32)
        keep = visual[...] == 0
        for k in range(0, width, 128):
            lanes = pl.ds(pl.multiple_of(b * width + k, 128), 128)
            words = embeds_ref[:, lanes].astype(F32)
            embeds_ref[:, lanes] = jnp.where(keep, words, placed[:, k:k + 128]).astype(BF16)

    def step(s, carry):
        @pl.when(s < blocks)
        def _():
            multiply(s)

        @pl.when((s >= skew) & (s < blocks + skew))
        def _():
            b = s - skew

            @pl.when(2 * d < n_dp)
            def _():
                pass_up(b)
                pass_down(b)

            @pl.when(2 * d >= n_dp)
            def _():
                pass_down(b)
                pass_up(b)

            finish(b)

        @pl.when(s == skew)
        def _():
            plan_landing()

        @pl.when(s > skew)
        def _():
            place(s - skew - 1)

        return carry

    lax.fori_loop(1, blocks + skew + 1, step, 0)

    def drain(b, carry):
        def up(i, c2):
            upward(b, d + 1 + i).wait_send()
            return c2
        lax.fori_loop(0, n_dp - 1 - d, up, 0)

        def down(c, c2):
            downward(b, c).wait_send()
            return c2
        lax.fori_loop(0, d, down, 0)
        for i in range(1, n_group):
            send_part(b, i).wait_send()
        return carry

    for i in range(1, n_tensor):
        send_rows(i).wait_send()
    for i in range(1, n_group):
        send_meta(i).wait_send()
    lax.fori_loop(0, blocks, drain, 0)


def per_device(hidden, out_weight, out_bias, text_embeds, image_rows, image_group, image_offset):
    n_group, n_dp, n_tensor = lax.axis_size("group"), lax.axis_size("dp"), lax.axis_size("tensor")
    depth, cols = out_weight.shape
    tokens = text_embeds.shape[0]
    all_rows = hidden.shape[0] * n_tensor
    rep = all_rows // n_dp
    width = min(WIDTH, cols)
    blocks = cols // width
    skew = min(SKEW, blocks)
    dma = lambda count: pltpu.SemaphoreType.DMA((count,))
    return pl.pallas_call(
        functools.partial(project_kernel, n_group, n_dp, n_tensor, width, skew),
        out_shape=pltpu.VMEM(text_embeds.shape, BF16),
        in_specs=[pl.BlockSpec(memory_space=pltpu.HBM)] * 7,
        out_specs=pl.BlockSpec(memory_space=pltpu.VMEM),
        scratch_shapes=[
            pltpu.SMEM(image_rows.shape, jnp.int32),
            pltpu.SMEM(image_group.shape, jnp.int32),
            pltpu.SMEM(image_offset.shape, jnp.int32),
            pltpu.VMEM(out_bias.shape, BF16),
            pltpu.VMEM((blocks, depth, width), BF16),
            pltpu.VMEM((all_rows, depth), BF16),
            pltpu.VMEM((blocks, n_dp, rep, width), BF16),
            pltpu.VMEM((blocks, n_dp + 1, rep, width), BF16),
            pltpu.VMEM((n_group * CAP, rep), BF16),
            pltpu.VMEM((blocks, n_group, CAP, width), BF16),
            pltpu.VMEM((blocks, n_group, CAP, width), BF16),
            pltpu.VMEM((n_group, 8, 128), jnp.int32),
            pltpu.VMEM((n_group, 8, 128), jnp.int32),
            pltpu.VMEM((tokens, n_group * CAP), BF16),
            pltpu.VMEM((tokens, 128), jnp.int32),
            dma(4), dma(blocks), dma(n_tensor), dma(n_tensor), pltpu.SemaphoreType.DMA,
            dma(blocks * n_dp), dma(blocks * n_dp), dma(blocks * n_dp), dma(blocks * n_dp),
            dma(blocks * n_group), dma(blocks * n_group), dma(n_group), dma(n_group),
            dma(blocks),
        ],
        compiler_params=pltpu.CompilerParams(
            collective_id=0, has_side_effects=True, vmem_limit_bytes=VMEM_MIB * 1024 * 1024
        ),
        cost_estimate=pl.CostEstimate(
            flops=2 * all_rows * depth * cols, bytes_accessed=2 * depth * cols, transcendentals=0
        ),
        name="project",
    )(image_rows, image_group, image_offset, hidden, out_weight, out_bias, text_embeds)


def solution(mesh):
    return jax.shard_map(
        per_device,
        mesh=mesh,
        in_specs=(
            P(("group", "tensor"), "dp"),
            P("dp", "tensor"),
            P("tensor"),
            P(("group", "dp"), "tensor"),
            P(("group", "dp"), None),
            P(("group", "dp"), None),
            P(("group", "dp"), None),
        ),
        out_specs=P(("group", "dp"), "tensor"),
        check_vma=False,
    )
```
